32 devices in a mesh: ax: 8 (over y, x, core), rad: 4 (over z).
Axes of the slice: x: 2, y: 2, z: 4, core: 2. Of those that a mesh axis runs over, the one named last changes fastest.
Arguments:
- couplings: bfloat16 [8, 6, 1728, 1728], P('ax', None, 'rad'), may hold values from -0.071777344 to 0.071777344
- pivots: float32 [8, 1728, 1728], P('ax', 'rad'), may hold values from -0.02946892 to 1.0294689
- pattern: int32 [8, 6, 9, 9], P('ax'), may hold values 0 or 1
- krylov: float32 [8, 32, 1728], P('ax', None, 'rad'), may hold values from -6 to 6
Outputs:
- basis_block: float32 [8, 16, 1728], P('ax', None, 'rad')
- coefficients: float32 [32, 16], replicated
- upper: float32 [16, 16], replicated
The draws below stay inside these ranges and needn't reach their ends.
All inputs are finite; a program needn't handle non-finite values. No bound on the sum of `pattern` on one device may be relied on, other than what follows from the above.
Results may differ from the reference program's by a relative error of at most 0.0003.
Values sent between devices are 32-bit elements; how exact they have to be, the bound alone decides.
A program may use at most 128 MiB of HBM per device.

```python
import jax
import jax.numpy as jnp
from jax import lax

FIELDS = 9
POINTS = 192
NRHS = 16
KRYLOV = 32
B = 1728
NB = 8
LEVELS = 3
ROWS = 13824


def draw_pivots(key, part):
    identity = jnp.eye(B, dtype=jnp.float32)
    limit = 1.225 / B ** 0.5
    noise = jax.random.normal(key, (NB, B, B), jnp.float32) * (0.7 / B ** 0.5)
    noise = jnp.clip(noise, -limit, limit)
    return identity[None] + noise


def plant(values, rng, low, top_value):
    place = [jax.random.randint(jax.random.fold_in(rng, axis), (), 0, length) for axis, length in enumerate(values.shape)]
    longest = values.shape.index(max(values.shape))
    neighbour = place[:longest] + [(place[longest] + 1) % values.shape[longest]] + place[longest + 1:]
    return values.at[tuple(place)].set(low).at[tuple(neighbour)].set(top_value)


def block_scale(own_key, dims, cuts, low, high):
    def one(axis_at, parts):
        steps = jax.random.uniform(jax.random.fold_in(jax.random.fold_in(own_key, 6), axis_at), (parts,), jnp.float32, low / len(cuts), high / len(cuts))
        return jnp.repeat(jnp.exp(steps), dims[axis_at] // parts).reshape((-1,) + (1,) * (len(dims) - axis_at - 1))

    gain = one(*cuts[0])
    for cut in cuts[1:]:
        gain = gain * one(*cut)
    return gain


def bell_draw(key, dims, spread, reach, cuts=(), held_as=jnp.bfloat16):
    drawn = jax.random.normal(key, dims, jnp.float32) * spread
    if len(cuts) > 0:
        drawn = block_scale(key, dims, cuts, -0.22, 0.18) * drawn
    return jnp.clip(drawn, min=-reach, max=reach).astype(held_as)


def setup_inputs(seed: int = 0) -> dict:
    seeds = jax.random.split(jax.random.key(seed), 5)
    couplings = bell_draw(seeds[0], (NB, 2 * LEVELS, B, B), (0.6 / B ** 0.5), 0.071777344, ((0, 8), (2, 4)))
    pivots = draw_pivots(jax.random.fold_in(seeds[4], 71), 0)
    pattern = plant((jax.random.randint(seeds[2], (NB, 2 * LEVELS, FIELDS, FIELDS), 0, 4) < 3).astype(jnp.int32), jax.random.fold_in(seeds[2], 1), 0, 1)
    krylov = bell_draw(seeds[3], (NB, KRYLOV, B), 1.0, 6.0, ((0, 8), (2, 4)), jnp.float32)
    return dict(couplings=couplings, pivots=pivots, pattern=pattern, krylov=krylov)


precise = lax.Precision.HIGHEST

def expand(mask):
    ones = mask.astype(jnp.float32)
    return jnp.repeat(jnp.repeat(ones, POINTS, axis=0), POINTS, axis=1)

def apply_factor(factor, vectors):
    return jnp.einsum('rc,kc->kr', factor, vectors, precision=precise)

def factor_of(couplings, pattern, block, kind):
    return couplings[block, kind].astype(jnp.float32) * expand(pattern[block, kind])

def reference(couplings, pivots, pattern, krylov):
    residue = krylov[:, KRYLOV - NRHS:, :]
    for rung in range(LEVELS):
        stride = 2 ** rung
        high = jnp.stack([apply_factor(factor_of(couplings, pattern, n, 2 * rung), residue[n]) for n in range(NB)])
        low = jnp.stack([apply_factor(factor_of(couplings, pattern, n, 2 * rung + 1), residue[n]) for n in range(NB)])
        zeros_pad = jnp.zeros((stride, NRHS, B), jnp.float32)
        from_below = jnp.concatenate([zeros_pad, high[:NB - stride]], axis=0)
        from_above = jnp.concatenate([low[stride:], zeros_pad], axis=0)
        residue = residue - from_below - from_above
    stacked = jnp.stack([apply_factor(pivots[n], residue[n]) for n in range(NB)])
    coefficients = jnp.einsum('nkb,nrb->kr', krylov, stacked, precision=precise) / ROWS
    remainder = stacked - jnp.einsum('kr,nkb->nrb', coefficients, krylov, precision=precise)
    gram = jnp.einsum('nrb,nsb->rs', remainder, remainder, precision=precise) / ROWS
    lower = jnp.linalg.cholesky(gram)
    flat = remainder.transpose(1, 0, 2).reshape(NRHS, NB * B)
    solved = lax.linalg.triangular_solve(lower, flat, left_side=True, lower=True)
    basis_block = solved.reshape(NRHS, NB, B).transpose(1, 0, 2)
    return (basis_block, coefficients, lower.T)
```

```python
import functools
import math

import jax
import jax.numpy as jnp
from jax import lax
from jax.experimental import pallas as pl
from jax.experimental.pallas import tpu as pltpu
from jax.sharding import PartitionSpec as P

NRHS = 16
SUBLANES = 8
LANES = 128
MESH = pl.DeviceIdType.MESH

precise = lax.Precision.HIGHEST


def dot_nt(a, b, precision=None):
    return lax.dot_general(
        a, b, (((1,), (1,)), ((), ())), precision=precision, preferred_element_type=jnp.float32
    )


def pack(matrix):
    groups = matrix.shape[0] // SUBLANES
    slot = LANES // groups
    parts = []
    for group in range(groups):
        parts.append(matrix[group * SUBLANES : (group + 1) * SUBLANES])
        if slot > matrix.shape[1]:
            parts.append(jnp.zeros((SUBLANES, slot - matrix.shape[1]), jnp.float32))
    return jnp.concatenate(parts, axis=1)


def unpack(tile, shape):
    groups = shape[0] // SUBLANES
    slot = LANES // groups
    return jnp.concatenate(
        [tile[:, group * slot : group * slot + shape[1]] for group in range(groups)], axis=0
    )


def halves(value):
    high = value.astype(jnp.bfloat16)
    low = (value - high.astype(jnp.float32)).astype(jnp.bfloat16)
    return high, low


def kernel(
    blocks, ranks, couplings, pivots, pattern, krylov, basis, coefficients, upper,
    factors, pivot_in, pivot_high, pivot_low, keep, pieces, inbox,
    tile_rad, tile_ax, load_sem, piece_send, piece_recv, push_send, push_recv,
    rad_send, rad_recv, ax_send, ax_recv,
):
    kinds, rows_here, width = factors.shape
    levels = kinds // 2
    stored_count = krylov.shape[1]
    fields = pattern.shape[3]
    points = width // fields
    rows_total = blocks * width
    me = lax.axis_index("ax")
    rank = lax.axis_index("rad")

    def load(kind):
        return pltpu.make_async_copy(couplings.at[0, kind], factors.at[kind], load_sem.at[kind])

    load_pivots = pltpu.make_async_copy(pivots.at[0], pivot_in, load_sem.at[kinds])
    for kind in range(kinds):
        load(kind).start()
    load_pivots.start()

    barrier = pltpu.get_barrier_semaphore()
    for step in range(1, ranks):
        pl.semaphore_signal(
            barrier, inc=1, device_id=(me, lax.rem(rank + step, ranks)), device_id_type=MESH
        )
    for step in range(1, blocks):
        pl.semaphore_signal(
            barrier, inc=1, device_id=(lax.rem(me + step, blocks), rank), device_id_type=MESH
        )
    pieces[0, rank] = krylov[0, stored_count - NRHS :, :]

    col_field = lax.broadcasted_iota(jnp.int32, (fields, width), 1) // points
    col_onehot = (col_field == lax.broadcasted_iota(jnp.int32, (fields, width), 0)).astype(
        jnp.float32
    )
    for kind in range(kinds):
        keep[kind] = jnp.dot(
            pattern[0, kind].astype(jnp.float32), col_onehot, preferred_element_type=jnp.float32
        )
    pl.semaphore_wait(barrier, ranks + blocks - 2)

    def piece_copy(level, step):
        return pltpu.make_async_remote_copy(
            src_ref=pieces.at[level, rank],
            dst_ref=pieces.at[level, rank],
            send_sem=piece_send.at[level, step],
            recv_sem=piece_recv.at[level, rank],
            device_id=(me, lax.rem(rank + step, ranks)),
            device_id_type=MESH,
        )

    def piece_arrival(level, step):
        source = lax.rem(rank + step, ranks)
        return pltpu.make_async_remote_copy(
            src_ref=pieces.at[level, source],
            dst_ref=pieces.at[level, source],
            send_sem=piece_send.at[level, step],
            recv_sem=piece_recv.at[level, source],
            device_id=(me, source),
            device_id_type=MESH,
        )

    def push_copy(level, way):
        stride = 1 << level
        target = me + stride if way == 0 else me - stride
        return pltpu.make_async_remote_copy(
            src_ref=inbox.at[level, 2 + way],
            dst_ref=inbox.at[level, way],
            send_sem=push_send.at[level, way],
            recv_sem=push_recv.at[level, way],
            device_id=(target, rank),
            device_id_type=MESH,
        )

    def rad_copy(which, step):
        return pltpu.make_async_remote_copy(
            src_ref=tile_rad.at[which, rank],
            dst_ref=tile_rad.at[which, rank],
            send_sem=rad_send.at[which, step],
            recv_sem=rad_recv.at[which, rank],
            device_id=(me, lax.rem(rank + step, ranks)),
            device_id_type=MESH,
        )

    def rad_arrival(which, step):
        source = lax.rem(rank + step, ranks)
        return pltpu.make_async_remote_copy(
            src_ref=tile_rad.at[which, source],
            dst_ref=tile_rad.at[which, source],
            send_sem=rad_send.at[which, step],
            recv_sem=rad_recv.at[which, source],
            device_id=(me, source),
            device_id_type=MESH,
        )

    def ax_copy(which, step):
        return pltpu.make_async_remote_copy(
            src_ref=tile_ax.at[which, me],
            dst_ref=tile_ax.at[which, me],
            send_sem=ax_send.at[which, step],
            recv_sem=ax_recv.at[which, me],
            device_id=(lax.rem(me + step, blocks), rank),
            device_id_type=MESH,
        )

    def ax_arrival(which, step):
        source = lax.rem(me + step, blocks)
        return pltpu.make_async_remote_copy(
            src_ref=tile_ax.at[which, source],
            dst_ref=tile_ax.at[which, source],
            send_sem=ax_send.at[which, step],
            recv_sem=ax_recv.at[which, source],
            device_id=(source, rank),
            device_id_type=MESH,
        )

    def send_pieces(level):
        for step in range(1, ranks):
            piece_copy(level, step).start()

    def whole(level):
        for step in range(1, ranks):
            piece_arrival(level, step).wait_recv()
        return jnp.concatenate([pieces[level, source] for source in range(ranks)], axis=1)

    def reduce_start(which, matrix):
        tile_rad[which, rank] = pack(matrix)
        for step in range(1, ranks):
            rad_copy(which, step).start()

    def reduce_middle(which):
        for step in range(1, ranks):
            rad_arrival(which, step).wait_recv()
        total = tile_rad[which, 0]
        for source in range(1, ranks):
            total += tile_rad[which, source]
        tile_ax[which, me] = total
        for step in range(1, blocks):
            ax_copy(which, step).start()

    def reduce_end(which, shape):
        for step in range(1, blocks):
            ax_arrival(which, step).wait_recv()
        total = tile_ax[which, 0]
        for source in range(1, blocks):
            total += tile_ax[which, source]
        return unpack(total, shape)

    group = math.gcd(points, rows_here)

    def mask(kind):
        load(kind).wait()

        @pl.loop(0, rows_here // group)
        def _(index):
            field = (rank * rows_here + index * group) // points
            row = keep[kind, pl.ds(field, 1), :]
            rows = pl.ds(pl.multiple_of(index * group, group), group)
            wide = jnp.broadcast_to(row, (group, width)).astype(jnp.bfloat16)
            factors[kind, rows, :] = factors[kind, rows, :] * wide

    def split_pivots():
        load_pivots.wait()

        @pl.loop(0, rows_here // group)
        def _(index):
            rows = pl.ds(pl.multiple_of(index * group, group), group)
            high, low = halves(pivot_in[rows, :])
            pivot_high[rows, :] = high
            pivot_low[rows, :] = low

    send_pieces(0)
    stored = krylov[0]
    reduce_start(0, dot_nt(stored, stored, precise))
    mask(0)
    mask(1)

    for level in range(levels):
        stride = 1 << level
        has_higher = me + stride < blocks
        has_lower = me >= stride
        both = jnp.concatenate(halves(whole(level)), axis=0)
        for way, has_target in ((0, has_higher), (1, has_lower)):
            product = dot_nt(both, factors[2 * level + way])
            inbox[level, 2 + way] = product[:NRHS] + product[NRHS:]

            @pl.when(has_target)
            def _():
                push_copy(level, way).start()

        if level + 1 < levels:
            mask(2 * level + 2)
        else:
            split_pivots()
        pieces[level + 1, rank] = pieces[level, rank]
        for way, has_source in ((0, has_lower), (1, has_higher)):

            @pl.when(has_source)
            def _():
                push_copy(level, way).wait_recv()
                pieces[level + 1, rank] = pieces[level + 1, rank] - inbox[level, way]

        send_pieces(level + 1)
        if level == 0:
            reduce_middle(0)
        if level + 1 < levels:
            mask(2 * level + 3)

    stored_gram = reduce_end(0, (stored_count, stored_count)) / rows_total
    diagonal = lax.broadcasted_iota(jnp.int32, (stored_count, stored_count), 0) == (
        lax.broadcasted_iota(jnp.int32, (stored_count, stored_count), 1)
    )
    middle = stored_gram - jnp.where(diagonal, 2.0, 0.0)

    high, low = halves(whole(levels))
    product = dot_nt(jnp.concatenate([high, low], axis=0), pivot_high[...])
    x = product[:NRHS] + product[NRHS:] + dot_nt(high, pivot_low[...])
    reduce_start(1, dot_nt(x, jnp.concatenate([stored, x], axis=0), precise))
    reduce_middle(1)
    sums = reduce_end(1, (NRHS, stored_count + NRHS)) / rows_total
    shares = sums[:, :stored_count]
    coefficients[...] = shares.T
    gram = sums[:, stored_count:] + dot_nt(
        jnp.dot(shares, middle, precision=precise, preferred_element_type=jnp.float32),
        shares,
        precise,
    )
    remainder = x - jnp.dot(shares, stored, precision=precise, preferred_element_type=jnp.float32)

    row_id = lax.broadcasted_iota(jnp.int32, (NRHS, 2 * NRHS), 0)
    col_id = lax.broadcasted_iota(jnp.int32, (NRHS, 2 * NRHS), 1)
    table = jnp.concatenate(
        [gram, (row_id == col_id)[:, :NRHS].astype(jnp.float32)], axis=1
    )
    for step in range(NRHS - 1):
        pivot_row = table[step : step + 1, :]
        factor = table[:, step : step + 1] / table[step : step + 1, step : step + 1]
        table = table - jnp.where(row_id > step, factor * pivot_row, 0.0)
    scale = jnp.sqrt(jnp.sum(jnp.where(row_id == col_id, table, 0.0), axis=1, keepdims=True))
    table = table / scale
    upper[...] = jnp.where(row_id <= col_id, table, 0.0)[:, :NRHS]
    basis[0] = jnp.dot(
        table[:, NRHS:], remainder, precision=precise, preferred_element_type=jnp.float32
    )

    for level in range(levels + 1):
        for step in range(1, ranks):
            piece_copy(level, step).wait_send()
    for level in range(levels):
        stride = 1 << level
        for way, has_target in ((0, me + stride < blocks), (1, me >= stride)):

            @pl.when(has_target)
            def _():
                push_copy(level, way).wait_send()

    for which in range(2):
        for step in range(1, ranks):
            rad_copy(which, step).wait_send()
        for step in range(1, blocks):
            ax_copy(which, step).wait_send()


def body(couplings, pivots, pattern, krylov):
    kinds, rows_here, width = couplings.shape[1:]
    blocks = lax.axis_size("ax")
    ranks = lax.axis_size("rad")
    fields = pattern.shape[3]
    levels = kinds // 2
    stored_count = krylov.shape[1]
    vmem = pl.BlockSpec(memory_space=pltpu.VMEM)
    hbm = pl.BlockSpec(memory_space=pl.ANY)
    dma = pltpu.SemaphoreType.DMA
    return pl.pallas_call(
        functools.partial(kernel, blocks, ranks),
        out_shape=(
            jax.ShapeDtypeStruct((1, NRHS, rows_here), jnp.float32),
            jax.ShapeDtypeStruct((stored_count, NRHS), jnp.float32),
            jax.ShapeDtypeStruct((NRHS, NRHS), jnp.float32),
        ),
        in_specs=[hbm, hbm, vmem, vmem],
        out_specs=(vmem, vmem, vmem),
        scratch_shapes=[
            pltpu.VMEM((kinds, rows_here, width), jnp.bfloat16),
            pltpu.VMEM((rows_here, width), jnp.float32),
            pltpu.VMEM((rows_here, width), jnp.bfloat16),
            pltpu.VMEM((rows_here, width), jnp.bfloat16),
            pltpu.VMEM((kinds, fields, width), jnp.float32),
            pltpu.VMEM((levels + 1, ranks, NRHS, rows_here), jnp.float32),
            pltpu.VMEM((levels, 4, NRHS, rows_here), jnp.float32),
            pltpu.VMEM((2, ranks, SUBLANES, LANES), jnp.float32),
            pltpu.VMEM((2, blocks, SUBLANES, LANES), jnp.float32),
            dma((kinds + 1,)),
            dma((levels + 1, ranks)),
            dma((levels + 1, ranks)),
            dma((levels, 2)),
            dma((levels, 2)),
            dma((2, ranks)),
            dma((2, ranks)),
            dma((2, blocks)),
            dma((2, blocks)),
        ],
        compiler_params=pltpu.CompilerParams(
            collective_id=0, has_side_effects=True, vmem_limit_bytes=48 * 1024 * 1024
        ),
    )(couplings, pivots, pattern, krylov)


def solution(mesh):
    return jax.shard_map(
        body,
        mesh=mesh,
        in_specs=(
            P("ax", None, "rad", None),
            P("ax", "rad", None),
            P("ax", None, None, None),
            P("ax", None, "rad"),
        ),
        out_specs=(P("ax", None, "rad"), P(), P()),
        check_vma=False,
    )
```

```python
import functools
import math

import jax
import jax.numpy as jnp
from jax import lax
from jax.experimental import pallas as pl
from jax.experimental.pallas import tpu as pltpu
from jax.sharding import PartitionSpec as P

NRHS = 16
SUBLANES = 8
LANES = 128
PART = 8
MESH = pl.DeviceIdType.MESH

precise = lax.Precision.HIGHEST


def dot_nt(a, b, precision=None):
    return lax.dot_general(
        a, b, (((1,), (1,)), ((), ())), precision=precision, preferred_element_type=jnp.float32
    )


def pack(matrix):
    groups = matrix.shape[0] // SUBLANES
    slot = LANES // groups
    parts = []
    for group in range(groups):
        parts.append(matrix[group * SUBLANES : (group + 1) * SUBLANES])
        if slot > matrix.shape[1]:
            parts.append(jnp.zeros((SUBLANES, slot - matrix.shape[1]), jnp.float32))
    return jnp.concatenate(parts, axis=1)


def unpack(tile, shape):
    groups = shape[0] // SUBLANES
    slot = LANES // groups
    return jnp.concatenate(
        [tile[:, group * slot : group * slot + shape[1]] for group in range(groups)], axis=0
    )


def halves(value):
    high = value.astype(jnp.bfloat16)
    low = (value - high.astype(jnp.float32)).astype(jnp.bfloat16)
    return high, low


def kernel(
    blocks, ranks, couplings, pivots, pattern_hbm, krylov_hbm, remainder_out, shares_out, table_out,
    pattern, krylov, factors, pivot_in, pivot_high, pivot_low, keep, pieces, inbox,
    tile_rad, tile_ax, load_sem, piece_send, piece_recv, push_send, push_recv,
    rad_send, rad_recv, ax_send, ax_recv,
):
    kinds, rows_here, width = factors.shape
    levels = kinds // 2
    parts = NRHS // PART
    stored_count = krylov.shape[1]
    fields = pattern.shape[3]
    points = width // fields
    rows_total = blocks * width
    me = lax.axis_index("ax")
    rank = lax.axis_index("rad")

    def load(kind):
        return pltpu.make_async_copy(couplings.at[0, kind], factors.at[kind], load_sem.at[kind])

    load_krylov = pltpu.make_async_copy(krylov_hbm, krylov, load_sem.at[kinds + 1])
    load_pattern = pltpu.make_async_copy(pattern_hbm, pattern, load_sem.at[kinds + 2])
    load_krylov.start()
    load_pattern.start()
    load_pivots = pltpu.make_async_copy(pivots.at[0], pivot_in, load_sem.at[kinds])
    for kind in range(2):
        load(kind).start()

    barrier = pltpu.get_barrier_semaphore()
    for step in range(1, ranks):
        pl.semaphore_signal(
            barrier, inc=1, device_id=(me, lax.rem(rank + step, ranks)), device_id_type=MESH
        )
    for step in range(1, blocks):
        pl.semaphore_signal(
            barrier, inc=1, device_id=(lax.rem(me + step, blocks), rank), device_id_type=MESH
        )
    load_krylov.wait()
    for part in range(parts):
        first = stored_count - NRHS + part * PART
        pieces[part, 0, rank] = krylov[0, first : first + PART, :]
    load_pattern.wait()

    col_field = lax.broadcasted_iota(jnp.int32, (fields, width), 1) // points
    col_onehot = (col_field == lax.broadcasted_iota(jnp.int32, (fields, width), 0)).astype(
        jnp.float32
    )
    for kind in range(kinds):
        keep[kind] = jnp.dot(
            pattern[0, kind].astype(jnp.float32), col_onehot, preferred_element_type=jnp.float32
        )
    pl.semaphore_wait(barrier, ranks + blocks - 2)

    def piece_copy(part, level, step):
        return pltpu.make_async_remote_copy(
            src_ref=pieces.at[part, level, rank],
            dst_ref=pieces.at[part, level, rank],
            send_sem=piece_send.at[part, level, step],
            recv_sem=piece_recv.at[part, level, rank],
            device_id=(me, lax.rem(rank + step, ranks)),
            device_id_type=MESH,
        )

    def piece_arrival(part, level, step):
        source = lax.rem(rank + step, ranks)
        return pltpu.make_async_remote_copy(
            src_ref=pieces.at[part, level, source],
            dst_ref=pieces.at[part, level, source],
            send_sem=piece_send.at[part, level, step],
            recv_sem=piece_recv.at[part, level, source],
            device_id=(me, source),
            device_id_type=MESH,
        )

    def push_copy(part, level, way):
        stride = 1 << level
        target = me + stride if way == 0 else me - stride
        return pltpu.make_async_remote_copy(
            src_ref=inbox.at[part, level, 2 + way],
            dst_ref=inbox.at[part, level, way],
            send_sem=push_send.at[part, level, way],
            recv_sem=push_recv.at[part, level, way],
            device_id=(target, rank),
            device_id_type=MESH,
        )

    def rad_copy(which, step):
        return pltpu.make_async_remote_copy(
            src_ref=tile_rad.at[which, rank],
            dst_ref=tile_rad.at[which, rank],
            send_sem=rad_send.at[which, step],
            recv_sem=rad_recv.at[which, rank],
            device_id=(me, lax.rem(rank + step, ranks)),
            device_id_type=MESH,
        )

    def rad_arrival(which, step):
        source = lax.rem(rank + step, ranks)
        return pltpu.make_async_remote_copy(
            src_ref=tile_rad.at[which, source],
            dst_ref=tile_rad.at[which, source],
            send_sem=rad_send.at[which, step],
            recv_sem=rad_recv.at[which, source],
            device_id=(me, source),
            device_id_type=MESH,
        )

    def ax_copy(which, step):
        return pltpu.make_async_remote_copy(
            src_ref=tile_ax.at[which, me],
            dst_ref=tile_ax.at[which, me],
            send_sem=ax_send.at[which, step],
            recv_sem=ax_recv.at[which, me],
            device_id=(lax.rem(me + step, blocks), rank),
            device_id_type=MESH,
        )

    def ax_arrival(which, step):
        source = lax.rem(me + step, blocks)
        return pltpu.make_async_remote_copy(
            src_ref=tile_ax.at[which, source],
            dst_ref=tile_ax.at[which, source],
            send_sem=ax_send.at[which, step],
            recv_sem=ax_recv.at[which, source],
            device_id=(source, rank),
            device_id_type=MESH,
        )

    def send_pieces(part, level):
        for step in range(1, ranks):
            piece_copy(part, level, step).start()

    def whole(part, level):
        for step in range(1, ranks):
            piece_arrival(part, level, step).wait_recv()
        return jnp.concatenate([pieces[part, level, source] for source in range(ranks)], axis=1)

    def reduce_start(which, matrix):
        tile_rad[which, rank] = pack(matrix)
        for step in range(1, ranks):
            rad_copy(which, step).start()

    def reduce_middle(which):
        for step in range(1, ranks):
            rad_arrival(which, step).wait_recv()
        total = tile_rad[which, 0]
        for source in range(1, ranks):
            total += tile_rad[which, source]
        tile_ax[which, me] = total
        for step in range(1, blocks):
            ax_copy(which, step).start()

    def reduce_end(which, shape):
        for step in range(1, blocks):
            ax_arrival(which, step).wait_recv()
        total = tile_ax[which, 0]
        for source in range(1, blocks):
            total += tile_ax[which, source]
        return unpack(total, shape)

    group = math.gcd(points, rows_here)

    def mask(kind):
        if kind != 1:
            load(kind).wait()

        @pl.loop(0, rows_here // group)
        def _(index):
            field = (rank * rows_here + index * group) // points
            row = keep[kind, pl.ds(field, 1), :]
            rows = pl.ds(pl.multiple_of(index * group, group), group)
            wide = jnp.broadcast_to(row, (group, width)).astype(jnp.bfloat16)
            factors[kind, rows, :] = factors[kind, rows, :] * wide

    def split_pivots():
        load_pivots.wait()

        @pl.loop(0, rows_here // group)
        def _(index):
            rows = pl.ds(pl.multiple_of(index * group, group), group)
            high, low = halves(pivot_in[rows, :])
            pivot_high[rows, :] = high
            pivot_low[rows, :] = low

    for part in range(parts):
        send_pieces(part, 0)
    stored = krylov[0]
    reduce_start(0, dot_nt(stored, stored, precise))
    load(1).wait()
    for kind in range(2, kinds):
        load(kind).start()
    load_pivots.start()
    mask(0)
    mask(1)

    for level in range(levels):
        stride = 1 << level
        has_higher = me + stride < blocks
        has_lower = me >= stride
        for part in range(parts):
            both = jnp.concatenate(halves(whole(part, level)), axis=0)
            for way, has_target in ((0, has_higher), (1, has_lower)):
                product = dot_nt(both, factors[2 * level + way])
                inbox[part, level, 2 + way] = product[:PART] + product[PART:]

                @pl.when(has_target)
                def _():
                    push_copy(part, level, way).start()

        if level + 1 < levels:
            mask(2 * level + 2)
        else:
            split_pivots()
        for part in range(parts):
            pieces[part, level + 1, rank] = pieces[part, level, rank]
            for way, has_source in ((0, has_lower), (1, has_higher)):

                @pl.when(has_source)
                def _():
                    push_copy(part, level, way).wait_recv()
                    pieces[part, level + 1, rank] = (
                        pieces[part, level + 1, rank] - inbox[part, level, way]
                    )

            send_pieces(part, level + 1)
        if level == 0:
            reduce_middle(0)
        if level + 1 < levels:
            mask(2 * level + 3)

    stored_gram = reduce_end(0, (stored_count, stored_count)) / rows_total
    diagonal = lax.broadcasted_iota(jnp.int32, (stored_count, stored_count), 0) == (
        lax.broadcasted_iota(jnp.int32, (stored_count, stored_count), 1)
    )
    middle = stored_gram - jnp.where(diagonal, 2.0, 0.0)

    solved = []
    for part in range(parts):
        high, low = halves(whole(part, levels))
        product = dot_nt(jnp.concatenate([high, low], axis=0), pivot_high[...])
        solved.append(product[:PART] + product[PART:] + dot_nt(high, pivot_low[...]))
    x = jnp.concatenate(solved, axis=0)
    reduce_start(1, dot_nt(x, jnp.concatenate([stored, x], axis=0), precise))
    reduce_middle(1)
    sums = reduce_end(1, (NRHS, stored_count + NRHS)) / rows_total
    shares = sums[:, :stored_count]
    shares_out[...] = shares
    gram = sums[:, stored_count:] + dot_nt(
        jnp.dot(shares, middle, precision=precise, preferred_element_type=jnp.float32),
        shares,
        precise,
    )
    remainder_out[...] = x - jnp.dot(shares, stored, precision=precise, preferred_element_type=jnp.float32)

    row_id = lax.broadcasted_iota(jnp.int32, (NRHS, 2 * NRHS), 0)
    col_id = lax.broadcasted_iota(jnp.int32, (NRHS, 2 * NRHS), 1)
    table = jnp.concatenate(
        [gram, (row_id == col_id)[:, :NRHS].astype(jnp.float32)], axis=1
    )
    for step in range(NRHS - 1):
        pivot_row = table[step : step + 1, :]
        factor = table[:, step : step + 1] / table[step : step + 1, step : step + 1]
        table = table - jnp.where(row_id > step, factor * pivot_row, 0.0)
    scale = jnp.sqrt(jnp.sum(jnp.where(row_id == col_id, table, 0.0), axis=1, keepdims=True))
    table = table / scale
    table_out[...] = table

    for part in range(parts):
        for level in range(levels + 1):
            for step in range(1, ranks):
                piece_copy(part, level, step).wait_send()
    for level in range(levels):
        stride = 1 << level
        for way, has_target in ((0, me + stride < blocks), (1, me >= stride)):

            @pl.when(has_target)
            def _():
                for part in range(parts):
                    push_copy(part, level, way).wait_send()

    for which in range(2):
        for step in range(1, ranks):
            rad_copy(which, step).wait_send()
        for step in range(1, blocks):
            ax_copy(which, step).wait_send()


def finish(remainder, shares, table, basis, shares_out, upper):
    values = table[...]
    row_id = lax.broadcasted_iota(jnp.int32, (NRHS, NRHS), 0)
    col_id = lax.broadcasted_iota(jnp.int32, (NRHS, NRHS), 1)
    upper[...] = jnp.where(row_id <= col_id, values[:, :NRHS], 0.0)
    shares_out[...] = shares[...]
    basis[0] = jnp.dot(
        values[:, NRHS:], remainder[...], precision=precise, preferred_element_type=jnp.float32
    )


def body(couplings, pivots, pattern, krylov):
    kinds, rows_here, width = couplings.shape[1:]
    blocks = lax.axis_size("ax")
    ranks = lax.axis_size("rad")
    fields = pattern.shape[3]
    levels = kinds // 2
    stored_count = krylov.shape[1]
    vmem = pl.BlockSpec(memory_space=pltpu.VMEM)
    hbm = pl.BlockSpec(memory_space=pl.ANY)
    dma = pltpu.SemaphoreType.DMA
    parts = NRHS // PART
    remainder, shares, table = pl.pallas_call(
        functools.partial(kernel, blocks, ranks),
        out_shape=(
            jax.ShapeDtypeStruct((NRHS, rows_here), jnp.float32),
            jax.ShapeDtypeStruct((NRHS, stored_count), jnp.float32),
            jax.ShapeDtypeStruct((NRHS, 2 * NRHS), jnp.float32),
        ),
        in_specs=[hbm, hbm, hbm, hbm],
        out_specs=(vmem, vmem, vmem),
        scratch_shapes=[
            pltpu.VMEM(pattern.shape, jnp.int32),
            pltpu.VMEM(krylov.shape, jnp.float32),
            pltpu.VMEM((kinds, rows_here, width), jnp.bfloat16),
            pltpu.VMEM((rows_here, width), jnp.float32),
            pltpu.VMEM((rows_here, width), jnp.bfloat16),
            pltpu.VMEM((rows_here, width), jnp.bfloat16),
            pltpu.VMEM((kinds, fields, width), jnp.float32),
            pltpu.VMEM((parts, levels + 1, ranks, PART, rows_here), jnp.float32),
            pltpu.VMEM((parts, levels, 4, PART, rows_here), jnp.float32),
            pltpu.VMEM((2, ranks, SUBLANES, LANES), jnp.float32),
            pltpu.VMEM((2, blocks, SUBLANES, LANES), jnp.float32),
            dma((kinds + 3,)),
            dma((parts, levels + 1, ranks)),
            dma((parts, levels + 1, ranks)),
            dma((parts, levels, 2)),
            dma((parts, levels, 2)),
            dma((2, ranks)),
            dma((2, ranks)),
            dma((2, blocks)),
            dma((2, blocks)),
        ],
        compiler_params=pltpu.CompilerParams(
            collective_id=0, has_side_effects=True, vmem_limit_bytes=60 * 1024 * 1024
        ),
    )(couplings, pivots, pattern, krylov)
    basis, shares, upper = pl.pallas_call(
        finish,
        out_shape=(
            jax.ShapeDtypeStruct((1, NRHS, rows_here), jnp.float32),
            jax.ShapeDtypeStruct((NRHS, stored_count), jnp.float32),
            jax.ShapeDtypeStruct((NRHS, NRHS), jnp.float32),
        ),
        in_specs=[vmem, vmem, vmem],
        out_specs=(vmem, vmem, vmem),
    )(remainder, shares, table)
    return basis, shares.T, upper


def solution(mesh):
    return jax.shard_map(
        body,
        mesh=mesh,
        in_specs=(
            P("ax", None, "rad", None),
            P("ax", "rad", None),
            P("ax", None, None, None),
            P("ax", None, "rad"),
        ),
        out_specs=(P("ax", None, "rad"), P(), P()),
        check_vma=False,
    )
```

```python
import functools
import math

import jax
import jax.numpy as jnp
from jax import lax
from jax.experimental import pallas as pl
from jax.experimental.pallas import tpu as pltpu
from jax.sharding import PartitionSpec as P

NRHS = 16
SUBLANES = 8
LANES = 128
PART = 8
MESH = pl.DeviceIdType.MESH

precise = lax.Precision.HIGHEST


def dot_nt(a, b, precision=None):
    return lax.dot_general(
        a, b, (((1,), (1,)), ((), ())), precision=precision, preferred_element_type=jnp.float32
    )


def pack(matrix):
    groups = matrix.shape[0] // SUBLANES
    slot = LANES // groups
    parts = []
    for group in range(groups):
        parts.append(matrix[group * SUBLANES : (group + 1) * SUBLANES])
        if slot > matrix.shape[1]:
            parts.append(jnp.zeros((SUBLANES, slot - matrix.shape[1]), jnp.float32))
    return jnp.concatenate(parts, axis=1)


def unpack(tile, shape):
    groups = shape[0] // SUBLANES
    slot = LANES // groups
    return jnp.concatenate(
        [tile[:, group * slot : group * slot + shape[1]] for group in range(groups)], axis=0
    )


def halves(value):
    high = value.astype(jnp.bfloat16)
    low = (value - high.astype(jnp.float32)).astype(jnp.bfloat16)
    return high, low


def kernel(
    blocks, ranks, couplings, pivots, pattern_hbm, krylov_hbm, remainder_out, shares_out, table_out,
    pattern, krylov, factors, pivot_in, pivot_high, pivot_low, keep, pieces, inbox,
    tile_rad, tile_ax, load_sem, piece_send, piece_recv, push_send, push_recv,
    rad_send, rad_recv, ax_send, ax_recv,
):
    kinds, rows_here, width = factors.shape
    levels = kinds // 2
    parts = NRHS // PART
    stored_count = krylov.shape[1]
    fields = pattern.shape[3]
    points = width // fields
    rows_total = blocks * width
    me = lax.axis_index("ax")
    rank = lax.axis_index("rad")

    def load(kind):
        return pltpu.make_async_copy(couplings.at[0, kind], factors.at[kind], load_sem.at[kind])

    load_krylov = pltpu.make_async_copy(krylov_hbm, krylov, load_sem.at[kinds + 1])
    load_pattern = pltpu.make_async_copy(pattern_hbm, pattern, load_sem.at[kinds + 2])
    load_krylov.start()
    load_pattern.start()
    load_pivots = pltpu.make_async_copy(pivots.at[0], pivot_in, load_sem.at[kinds])
    for kind in range(2):
        load(kind).start()

    barrier = pltpu.get_barrier_semaphore()
    for step in range(1, ranks):
        pl.semaphore_signal(
            barrier, inc=1, device_id=(me, lax.rem(rank + step, ranks)), device_id_type=MESH
        )
    for step in range(1, blocks):
        pl.semaphore_signal(
            barrier, inc=1, device_id=(lax.rem(me + step, blocks), rank), device_id_type=MESH
        )
    load_krylov.wait()
    for part in range(parts):
        first = stored_count - NRHS + part * PART
        pieces[part, 0, rank] = krylov[0, first : first + PART, :]
    load_pattern.wait()

    col_field = lax.broadcasted_iota(jnp.int32, (fields, width), 1) // points
    col_onehot = (col_field == lax.broadcasted_iota(jnp.int32, (fields, width), 0)).astype(
        jnp.float32
    )
    for kind in range(kinds):
        keep[kind] = jnp.dot(
            pattern[kind, :, 0, :].astype(jnp.float32), col_onehot, preferred_element_type=jnp.float32
        )
    pl.semaphore_wait(barrier, ranks + blocks - 2)

    def piece_copy(part, level, step):
        return pltpu.make_async_remote_copy(
            src_ref=pieces.at[part, level, rank],
            dst_ref=pieces.at[part, level, rank],
            send_sem=piece_send.at[part, level, step],
            recv_sem=piece_recv.at[part, level, rank],
            device_id=(me, lax.rem(rank + step, ranks)),
            device_id_type=MESH,
        )

    def piece_arrival(part, level, step):
        source = lax.rem(rank + step, ranks)
        return pltpu.make_async_remote_copy(
            src_ref=pieces.at[part, level, source],
            dst_ref=pieces.at[part, level, source],
            send_sem=piece_send.at[part, level, step],
            recv_sem=piece_recv.at[part, level, source],
            device_id=(me, source),
            device_id_type=MESH,
        )

    def push_copy(part, level, way):
        stride = 1 << level
        target = me + stride if way == 0 else me - stride
        return pltpu.make_async_remote_copy(
            src_ref=inbox.at[part, level, 2 + way],
            dst_ref=inbox.at[part, level, way],
            send_sem=push_send.at[part, level, way],
            recv_sem=push_recv.at[part, level, way],
            device_id=(target, rank),
            device_id_type=MESH,
        )

    def rad_copy(which, step):
        return pltpu.make_async_remote_copy(
            src_ref=tile_rad.at[which, rank],
            dst_ref=tile_rad.at[which, rank],
            send_sem=rad_send.at[which, step],
            recv_sem=rad_recv.at[which, rank],
            device_id=(me, lax.rem(rank + step, ranks)),
            device_id_type=MESH,
        )

    def rad_arrival(which, step):
        source = lax.rem(rank + step, ranks)
        return pltpu.make_async_remote_copy(
            src_ref=tile_rad.at[which, source],
            dst_ref=tile_rad.at[which, source],
            send_sem=rad_send.at[which, step],
            recv_sem=rad_recv.at[which, source],
            device_id=(me, source),
            device_id_type=MESH,
        )

    def ax_copy(which, step):
        return pltpu.make_async_remote_copy(
            src_ref=tile_ax.at[which, me],
            dst_ref=tile_ax.at[which, me],
            send_sem=ax_send.at[which, step],
            recv_sem=ax_recv.at[which, me],
            device_id=(lax.rem(me + step, blocks), rank),
            device_id_type=MESH,
        )

    def ax_arrival(which, step):
        source = lax.rem(me + step, blocks)
        return pltpu.make_async_remote_copy(
            src_ref=tile_ax.at[which, source],
            dst_ref=tile_ax.at[which, source],
            send_sem=ax_send.at[which, step],
            recv_sem=ax_recv.at[which, source],
            device_id=(source, rank),
            device_id_type=MESH,
        )

    def send_pieces(part, level):
        for step in range(1, ranks):
            piece_copy(part, level, step).start()

    def whole(part, level):
        for step in range(1, ranks):
            piece_arrival(part, level, step).wait_recv()
        return jnp.concatenate([pieces[part, level, source] for source in range(ranks)], axis=1)

    def reduce_start(which, matrix):
        tile_rad[which, rank] = pack(matrix)
        for step in range(1, ranks):
            rad_copy(which, step).start()

    def reduce_middle(which):
        for step in range(1, ranks):
            rad_arrival(which, step).wait_recv()
        total = tile_rad[which, 0]
        for source in range(1, ranks):
            total += tile_rad[which, source]
        tile_ax[which, me] = total
        for step in range(1, blocks):
            ax_copy(which, step).start()

    def reduce_end(which, shape):
        for step in range(1, blocks):
            ax_arrival(which, step).wait_recv()
        total = tile_ax[which, 0]
        for source in range(1, blocks):
            total += tile_ax[which, source]
        return unpack(total, shape)

    group = math.gcd(points, rows_here)

    def mask(kind):
        if kind != 1:
            load(kind).wait()

        @pl.loop(0, rows_here // group)
        def _(index):
            field = (rank * rows_here + index * group) // points
            row = keep[kind, pl.ds(field, 1), :]
            rows = pl.ds(pl.multiple_of(index * group, group), group)
            wide = jnp.broadcast_to(row, (group, width)).astype(jnp.bfloat16)
            factors[kind, rows, :] = factors[kind, rows, :] * wide

    def split_pivots():
        load_pivots.wait()

        @pl.loop(0, rows_here // group)
        def _(index):
            rows = pl.ds(pl.multiple_of(index * group, group), group)
            high, low = halves(pivot_in[rows, :])
            pivot_high[rows, :] = high
            pivot_low[rows, :] = low

    for part in range(parts):
        send_pieces(part, 0)
    stored = krylov[0]
    reduce_start(0, dot_nt(stored, stored, precise))
    load(1).wait()
    for kind in range(2, kinds):
        load(kind).start()
    load_pivots.start()
    mask(0)
    mask(1)

    for level in range(levels):
        stride = 1 << level
        has_higher = me + stride < blocks
        has_lower = me >= stride
        for part in range(parts):
            both = jnp.concatenate(halves(whole(part, level)), axis=0)
            for way, has_target in ((0, has_higher), (1, has_lower)):
                product = dot_nt(both, factors[2 * level + way])
                inbox[part, level, 2 + way] = product[:PART] + product[PART:]

                @pl.when(has_target)
                def _():
                    push_copy(part, level, way).start()

        if level + 1 < levels:
            mask(2 * level + 2)
        else:
            split_pivots()
        for part in range(parts):
            pieces[part, level + 1, rank] = pieces[part, level, rank]
            for way, has_source in ((0, has_lower), (1, has_higher)):

                @pl.when(has_source)
                def _():
                    push_copy(part, level, way).wait_recv()
                    pieces[part, level + 1, rank] = (
                        pieces[part, level + 1, rank] - inbox[part, level, way]
                    )

            send_pieces(part, level + 1)
        if level == 0:
            reduce_middle(0)
        if level + 1 < levels:
            mask(2 * level + 3)

    stored_gram = reduce_end(0, (stored_count, stored_count)) / rows_total
    diagonal = lax.broadcasted_iota(jnp.int32, (stored_count, stored_count), 0) == (
        lax.broadcasted_iota(jnp.int32, (stored_count, stored_count), 1)
    )
    middle = stored_gram - jnp.where(diagonal, 2.0, 0.0)

    solved = []
    for part in range(parts):
        high, low = halves(whole(part, levels))
        product = dot_nt(jnp.concatenate([high, low], axis=0), pivot_high[...])
        solved.append(product[:PART] + product[PART:] + dot_nt(high, pivot_low[...]))
    x = jnp.concatenate(solved, axis=0)
    reduce_start(1, dot_nt(x, jnp.concatenate([stored, x], axis=0), precise))
    reduce_middle(1)
    sums = reduce_end(1, (NRHS, stored_count + NRHS)) / rows_total
    shares = sums[:, :stored_count]
    shares_out[...] = shares
    gram = sums[:, stored_count:] + dot_nt(
        jnp.dot(shares, middle, precision=precise, preferred_element_type=jnp.float32),
        shares,
        precise,
    )
    remainder_out[...] = x - jnp.dot(shares, stored, precision=precise, preferred_element_type=jnp.float32)

    row_id = lax.broadcasted_iota(jnp.int32, (NRHS, 2 * NRHS), 0)
    col_id = lax.broadcasted_iota(jnp.int32, (NRHS, 2 * NRHS), 1)
    table = jnp.concatenate(
        [gram, (row_id == col_id)[:, :NRHS].astype(jnp.float32)], axis=1
    )
    for step in range(NRHS - 1):
        pivot_row = table[step : step + 1, :]
        factor = table[:, step : step + 1] / table[step : step + 1, step : step + 1]
        table = table - jnp.where(row_id > step, factor * pivot_row, 0.0)
    scale = jnp.sqrt(jnp.sum(jnp.where(row_id == col_id, table, 0.0), axis=1, keepdims=True))
    table = table / scale
    table_out[...] = table

    for part in range(parts):
        for level in range(levels + 1):
            for step in range(1, ranks):
                piece_copy(part, level, step).wait_send()
    for level in range(levels):
        stride = 1 << level
        for way, has_target in ((0, me + stride < blocks), (1, me >= stride)):

            @pl.when(has_target)
            def _():
                for part in range(parts):
                    push_copy(part, level, way).wait_send()

    for which in range(2):
        for step in range(1, ranks):
            rad_copy(which, step).wait_send()
        for step in range(1, blocks):
            ax_copy(which, step).wait_send()


def finish(remainder, shares, table, basis, shares_out, upper):
    values = table[...]
    row_id = lax.broadcasted_iota(jnp.int32, (NRHS, NRHS), 0)
    col_id = lax.broadcasted_iota(jnp.int32, (NRHS, NRHS), 1)
    upper[...] = jnp.where(row_id <= col_id, values[:, :NRHS], 0.0)
    shares_out[...] = shares[...]
    basis[0] = jnp.dot(
        values[:, NRHS:], remainder[...], precision=precise, preferred_element_type=jnp.float32
    )


def body(couplings, pivots, pattern, krylov):
    kinds, rows_here, width = couplings.shape[1:]
    blocks = lax.axis_size("ax")
    ranks = lax.axis_size("rad")
    fields = pattern.shape[3]
    levels = kinds // 2
    stored_count = krylov.shape[1]
    vmem = pl.BlockSpec(memory_space=pltpu.VMEM)
    hbm = pl.BlockSpec(memory_space=pl.ANY)
    dma = pltpu.SemaphoreType.DMA
    parts = NRHS // PART
    remainder, shares, table = pl.pallas_call(
        functools.partial(kernel, blocks, ranks),
        out_shape=(
            jax.ShapeDtypeStruct((NRHS, rows_here), jnp.float32),
            jax.ShapeDtypeStruct((NRHS, stored_count), jnp.float32),
            jax.ShapeDtypeStruct((NRHS, 2 * NRHS), jnp.float32),
        ),
        in_specs=[hbm, hbm, hbm, hbm],
        out_specs=(vmem, vmem, vmem),
        scratch_shapes=[
            pltpu.VMEM((kinds, fields, 1, fields), jnp.int32),
            pltpu.VMEM(krylov.shape, jnp.float32),
            pltpu.VMEM((kinds, rows_here, width), jnp.bfloat16),
            pltpu.VMEM((rows_here, width), jnp.float32),
            pltpu.VMEM((rows_here, width), jnp.bfloat16),
            pltpu.VMEM((rows_here, width), jnp.bfloat16),
            pltpu.VMEM((kinds, fields, width), jnp.float32),
            pltpu.VMEM((parts, levels + 1, ranks, PART, rows_here), jnp.float32),
            pltpu.VMEM((parts, levels, 4, PART, rows_here), jnp.float32),
            pltpu.VMEM((2, ranks, SUBLANES, LANES), jnp.float32),
            pltpu.VMEM((2, blocks, SUBLANES, LANES), jnp.float32),
            dma((kinds + 3,)),
            dma((parts, levels + 1, ranks)),
            dma((parts, levels + 1, ranks)),
            dma((parts, levels, 2)),
            dma((parts, levels, 2)),
            dma((2, ranks)),
            dma((2, ranks)),
            dma((2, blocks)),
            dma((2, blocks)),
        ],
        compiler_params=pltpu.CompilerParams(
            collective_id=0, has_side_effects=True, vmem_limit_bytes=60 * 1024 * 1024
        ),
    )(couplings, pivots, pattern.transpose(1, 2, 0, 3), krylov)
    basis, shares, upper = pl.pallas_call(
        finish,
        out_shape=(
            jax.ShapeDtypeStruct((1, NRHS, rows_here), jnp.float32),
            jax.ShapeDtypeStruct((NRHS, stored_count), jnp.float32),
            jax.ShapeDtypeStruct((NRHS, NRHS), jnp.float32),
        ),
        in_specs=[vmem, vmem, vmem],
        out_specs=(vmem, vmem, vmem),
    )(remainder, shares, table)
    return basis, shares.T, upper


def solution(mesh):
    return jax.shard_map(
        body,
        mesh=mesh,
        in_specs=(
            P("ax", None, "rad", None),
            P("ax", "rad", None),
            P("ax", None, None, None),
            P("ax", None, "rad"),
        ),
        out_specs=(P("ax", None, "rad"), P(), P()),
        check_vma=False,
    )
```
